256 devices in a mesh: mem: 8 (over y, z_hi), samp: 32 (over x, z_lo, core).
Axes of the slice: x: 4, y: 4, z: 8 (z_hi: 2, z_lo: 4; z = z_hi * 4 + z_lo), core: 2. Of those that a mesh axis runs over, the one named last changes fastest.
Arguments:
- first_plane: bfloat16 [65536, 16384], P('samp', 'mem')
- second_plane: bfloat16 [16384, 16384], P('samp', 'mem')
- panel_owner: int32 [2], replicated, may hold values from 0 to 31
Outputs:
- covariance: float32 [1024, 65536], P('mem', 'samp')
The draws below stay inside these ranges and needn't reach their ends.
All inputs are finite; a program needn't handle non-finite values.
Results may differ from the reference program's by a relative error of at most 0.0004.
The reference program's roundings to bfloat16 on the way count: a program that leaves them out, or rounds other values in their place, can miss the bound.
Values may be sent and summed in bfloat16 or wider, within the bound.
No kernel may reach another device: no remote copies, remote signals or barrier semaphores. Data moves between devices by JAX's collectives and lax.ppermute only.
A program may use at most 64 MiB of HBM per device.

```python
import jax
import jax.numpy as jnp
from jax import lax

ROWS_DEV = 2048
PANEL = 512
SAMPLES = 65536
MEMBERS = 16384
Y_ROWS = 16384
N_SAMP = 32


def plane_draw(key, rows):
    key_mean, key_scale, key_noise = jax.random.split(key, 3)
    centre = 3.0 * jax.random.normal(key_mean, (rows, 1), jnp.float32)
    noise = jax.random.normal(key_noise, (rows, MEMBERS), jnp.float32)
    spread = jnp.exp(jax.random.uniform(key_scale, (rows, 1), jnp.float32, 1.386, 2.996))
    weight = 0.5 + jnp.arange(MEMBERS, dtype=jnp.float32)[None, :] / MEMBERS
    return (centre * weight + spread * noise).astype(jnp.bfloat16)


def draw_first_plane(key, part):
    return plane_draw(jax.random.fold_in(key, 11), SAMPLES)


def draw_second_plane(key, part):
    return plane_draw(jax.random.fold_in(key, 23), Y_ROWS)


def setup_inputs(seed: int = 0) -> dict:
    key_of = jax.random.split(jax.random.key(seed), 4)
    return {
        "first_plane": draw_first_plane(jax.random.fold_in(key_of[3], 71), 0),
        "second_plane": draw_second_plane(jax.random.fold_in(key_of[3], 71), 0),
        "panel_owner": jax.random.randint(key_of[2], (2,), 0, N_SAMP).astype(jnp.int32),
    }


def reference(first_plane, second_plane, panel_owner):
    first_panel = lax.dynamic_slice_in_dim(second_plane, (panel_owner[0] * PANEL).astype(jnp.int32), PANEL, 0)
    second_panel = lax.dynamic_slice_in_dim(second_plane, (panel_owner[1] * PANEL).astype(jnp.int32), PANEL, 0)
    panels = jnp.concatenate([first_panel, second_panel], axis=0).astype(jnp.float32)
    panel_mean = jnp.sum(panels, axis=1) / MEMBERS
    panel_anom = (panels - panel_mean[:, None]).astype(jnp.bfloat16)
    blocks = first_plane.reshape(SAMPLES // ROWS_DEV, ROWS_DEV, MEMBERS)

    def one_block(rows):
        wide = rows.astype(jnp.float32)
        row_mean = jnp.sum(wide, axis=1) / MEMBERS
        anomaly = (wide - row_mean[:, None]).astype(jnp.bfloat16)
        product = lax.dot_general(panel_anom, anomaly, (((1,), (1,)), ((), ())), preferred_element_type=jnp.float32)
        return product / (MEMBERS - 1)

    result = lax.map(one_block, blocks)
    return jnp.transpose(result, (1, 0, 2)).reshape(2 * PANEL, SAMPLES)
```

```python
import jax
import jax.numpy as jnp
from jax import lax
from jax.sharding import PartitionSpec as P

F32 = jnp.float32
BF16 = jnp.bfloat16
WIRE = jnp.float16
CHUNKS = 2


def swap(value, axis, bits):
    size = lax.axis_size(axis)
    return lax.ppermute(value, axis, [(i, i ^ bits) for i in range(size)])


def pick(index, options):
    result = options[-1]
    for i in range(len(options) - 2, -1, -1):
        result = jnp.where(index == i, options[i], result)
    return result


def row_stats(rows):
    wide = rows.astype(F32)
    return jnp.stack([jnp.sum(wide, -1), jnp.max(wide, -1), jnp.max(-wide, -1)])


def merge(parts):
    total = parts[0]
    for part in parts[1:]:
        total = jnp.concatenate([total[:1] + part[:1], jnp.maximum(total[1:], part[1:])])
    return total


def over_members(stats):
    stats = merge([stats] + [swap(stats, "mem", bits) for bits in (2, 4, 6)])
    return merge([stats, swap(stats, "mem", 1)])


def mean_and_reach(stats, members):
    mean = stats[0] / members
    return mean, jnp.maximum(stats[1] - mean, stats[2] + mean)


def per_device(first_plane, second_plane, panel_owner):
    members = first_plane.shape[1] * lax.axis_size("mem")
    shard = first_plane.shape[1]
    samp, mem = lax.axis_index("samp"), lax.axis_index("mem")
    my_x, my_z, my_core = samp // 8, (samp // 2) % 4, samp % 2
    my_y, my_zh = mem // 2, mem % 2
    own_x, own_z, own_core = panel_owner // 8, (panel_owner // 2) % 4, panel_owner % 2

    eighth = 64 // 8 // CHUNKS * 2
    by_x = second_plane.reshape(4, 128, shard)
    piece = lambda bits: lax.dynamic_index_in_dim(by_x, my_x ^ bits, 0, keepdims=False)
    from_x = [piece(0)] + [swap(piece(bits), "samp", 8 * bits) for bits in (1, 2, 3)]
    halves = [
        pick(my_x ^ own_x[p], from_x).reshape(CHUNKS, 2, 4, eighth, shard) for p in range(2)
    ]
    half = lambda core: jnp.stack(
        [lax.dynamic_index_in_dim(h, core, 1, keepdims=False) for h in halves]
    )
    kept, got = half(my_core), swap(half(1 - my_core), "samp", 1)
    quarters = jnp.stack(
        [jnp.where(my_core == own_core[p], kept[p], got[p]) for p in range(2)]
    )
    piece_z = lambda bits: lax.dynamic_index_in_dim(quarters, my_z ^ bits, 2, keepdims=False)
    from_z = [piece_z(0)] + [swap(piece_z(bits), "samp", 2 * bits) for bits in (1, 2, 3)]
    mine = jnp.stack([pick(my_z ^ own_z[p], [f[p] for f in from_z]) for p in range(2)])

    first_mean, first_reach = mean_and_reach(over_members(row_stats(first_plane)), members)
    panel_facts = jnp.stack(
        mean_and_reach(over_members(row_stats(mine).reshape(3, -1)), members)
    ).reshape(2, 2, CHUNKS, eighth)

    def along_z(value, axis):
        parts = [value] + [swap(value, "samp", 2 * bits) for bits in (1, 2, 3)]
        return jnp.stack([pick(my_z ^ place, parts) for place in range(4)], axis)

    def along_x(value):
        return jnp.stack([value] + [swap(value, "samp", 8 * bits) for bits in (1, 2, 3)])

    def along_core(value, axis):
        other = swap(value, "samp", 1)
        return jnp.stack(
            [jnp.where(my_core == 0, value, other), jnp.where(my_core == 0, other, value)], axis
        )

    facts = along_core(along_x(along_z(panel_facts, 3)), 4)
    line = along_z(mine, 2)
    panel_reach = jnp.max(facts[:, 1])
    shrink_first = 4.0 / jnp.maximum(jnp.max(first_reach), 1e-30)
    shrink_panel = 1.0 / jnp.maximum(panel_reach, 1e-30)
    grow_first, grow_panel = 1.0 / shrink_first, 1.0 / shrink_panel

    first_anom = (first_plane.astype(F32) - first_mean[:, None]).astype(BF16)
    rows = 4 * 2 * eighth
    results = []
    for chunk in range(CHUNKS):
        panels = along_core(along_x(line[:, chunk]), 2)
        panel_mean = facts[:, 0, :, chunk]
        panel_anom = (panels.astype(F32) - panel_mean[..., None]).astype(BF16)
        shares = lax.dot_general(
            panel_anom.reshape(8 * rows, shard),
            first_anom,
            (((1,), (1,)), ((), ())),
            preferred_element_type=F32,
        ).reshape(2, 2, 2, rows, -1)

        def for_y(dest):
            return lax.dynamic_slice(
                shares,
                ((dest % 2) ^ (my_x // 2), 0, dest // 2, 0, 0),
                (1, 2, 1, rows, shares.shape[-1]),
            ).reshape(2, rows, -1)

        total = for_y(my_y)
        for bits in (1, 2, 3):
            sent = (for_y(my_y ^ bits) * shrink_first * shrink_panel).astype(WIRE)
            total += swap(sent, "mem", 2 * bits).astype(F32) * grow_panel * grow_first
        for_z = lambda dest: lax.dynamic_index_in_dim(total, dest ^ (my_x % 2), 0, keepdims=False)
        sent = (for_z(1 - my_zh) * shrink_first * shrink_panel).astype(WIRE)
        total = for_z(my_zh) + swap(sent, "mem", 1).astype(F32) * grow_panel * grow_first
        results.append(total / (members - 1))
    return jnp.concatenate(results, axis=0)


def solution(mesh):
    in_specs = (P("samp", "mem"), P("samp", "mem"), P())
    out_specs = P("mem", "samp")
    return jax.shard_map(
        per_device, mesh=mesh, in_specs=in_specs, out_specs=out_specs, check_vma=False
    )
```

```python
import jax
import jax.numpy as jnp
from jax import lax
from jax.sharding import PartitionSpec as P

F32 = jnp.float32
BF16 = jnp.bfloat16
WIRE = jnp.float16
CHUNKS = 2


def swap(value, axis, bits):
    size = lax.axis_size(axis)
    return lax.ppermute(value, axis, [(i, i ^ bits) for i in range(size)])


def pick(index, options):
    result = options[-1]
    for i in range(len(options) - 2, -1, -1):
        result = jnp.where(index == i, options[i], result)
    return result


def row_stats(rows):
    wide = rows.astype(F32)
    return jnp.stack([jnp.sum(wide, -1), jnp.max(wide, -1), jnp.max(-wide, -1)])


def merge(parts):
    total = parts[0]
    for part in parts[1:]:
        total = jnp.concatenate([total[:1] + part[:1], jnp.maximum(total[1:], part[1:])])
    return total


def after(value, others):
    return lax.optimization_barrier((value, others))[0]


def per_device(first_plane, second_plane, panel_owner):
    samples, shard = first_plane.shape
    members = shard * lax.axis_size("mem")
    samp, mem = lax.axis_index("samp"), lax.axis_index("mem")
    my_x, my_z, my_core = samp >> 3, (samp >> 1) & 3, samp & 1
    my_y, my_zh = mem >> 1, mem & 1
    own_x, own_z, own_core = panel_owner >> 3, (panel_owner >> 1) & 3, panel_owner & 1

    by_x = second_plane.reshape(4, 128, shard)
    piece = lambda bits: lax.dynamic_index_in_dim(by_x, my_x ^ bits, 0, keepdims=False)
    from_x = [piece(0)] + [swap(piece(bits), "samp", 8 * bits) for bits in (1, 2, 3)]
    first_plane = after(first_plane, from_x[0])
    first_local = row_stats(first_plane)
    halves = [
        pick(my_x ^ own_x[p], from_x).reshape(CHUNKS, 2, 4, -1, shard) for p in range(2)
    ]
    half = lambda core: jnp.stack(
        [lax.dynamic_index_in_dim(h, core, 1, keepdims=False) for h in halves]
    )
    kept, got = half(my_core), swap(half(1 - my_core), "samp", 1)
    column = jnp.stack(
        [jnp.where(my_core == own_core[p], kept[p], got[p]) for p in range(2)]
    )
    eighth = column.shape[3]
    piece_z = lambda bits: lax.dynamic_index_in_dim(column, my_z ^ bits, 2, keepdims=False)
    from_z = [piece_z(0)] + [swap(piece_z(bits), "samp", 2 * bits) for bits in (1, 2, 3)]

    column_local = row_stats(column).reshape(3, -1)
    stats = jnp.concatenate([first_local, column_local], axis=1)
    stats = merge([stats] + [swap(stats, "mem", bits) for bits in (2, 4, 6)])
    stats = after(stats, from_z[1:])
    stats = merge([stats, swap(stats, "mem", 1)])
    mean, span = stats[0] / members, stats[1] + stats[2]
    first_mean = mean[:samples]
    facts = jnp.stack([mean[samples:], span[samples:]]).reshape((2,) + column.shape[:-1])

    mine = jnp.stack([pick(my_z ^ own_z[p], [f[p] for f in from_z]) for p in range(2)])
    parts = [mine] + [swap(mine, "samp", 2 * bits) for bits in (1, 2, 3)]
    facts = after(facts, parts[1])
    facts_z = [facts] + [swap(facts, "samp", 2 * bits) for bits in (1, 2, 3)]
    facts = jnp.stack([pick(my_z ^ own_z[p], [f[:, p] for f in facts_z]) for p in range(2)], 1)
    line = jnp.stack([pick(my_z ^ place, parts) for place in range(4)], 2)
    line = (line.astype(F32) - facts[0][..., None]).astype(BF16)
    tiles = 8
    bound = jnp.max(facts[1]) * 1.02
    mark = jnp.broadcast_to(bound, (1, eighth, shard)).astype(BF16)

    first_anom = (first_plane.astype(F32) - first_mean[:, None]).astype(BF16)
    rows = 4 * eighth
    gathered = []
    for chunk in range(CHUNKS):
        sent = line[:, chunk].reshape(tiles, eighth, shard)
        if chunk == 0:
            sent = jnp.concatenate([sent, mark])
        else:
            sent = after(sent, gathered[0][1])
        gathered.append([sent] + [swap(sent, "samp", 8 * bits) for bits in (1, 2, 3)])

    blocks, arrived = [], []
    for chunk in range(CHUNKS):
        if chunk > 0:
            gathered[chunk] = after(gathered[chunk], arrived[-1][0])
        near = jnp.stack(gathered[chunk])
        far = swap(near, "samp", 1)
        if chunk == 0:
            marks = jnp.stack([near[:, tiles, 0, :128], far[:, tiles, 0, :128]])
            shrink_first = 4.0 / jnp.maximum(jnp.max(span[:samples]), 1e-30)
            shrink_panel = 1.0 / jnp.maximum(jnp.max(marks.astype(F32)), 1e-30)
            grow_first, grow_panel = 1.0 / shrink_first, 1.0 / shrink_panel
        panel_anom = jnp.stack([near[:, :tiles], far[:, :tiles]])
        shares = lax.dot_general(
            panel_anom.reshape(16 * rows, shard),
            first_anom,
            (((1,), (1,)), ((), ())),
            preferred_element_type=F32,
        ).reshape(2, 2, 2, 2, rows, samples)

        def for_y(dest):
            start = (0, (dest & 1) ^ (my_x >> 1), 0, dest >> 1, 0, 0)
            block = lax.dynamic_slice(shares, start, (2, 1, 2, 1, rows, samples))
            return block.reshape(2, 2, rows, samples)

        sent = [
            (for_y(my_y ^ bits) * shrink_first * shrink_panel).astype(WIRE) for bits in (1, 2, 3)
        ]
        arrived.append([swap(sent[bits - 1], "mem", 2 * bits) for bits in (1, 2, 3)])
        blocks.append(for_y(my_y))

    results = []
    for chunk in range(CHUNKS):
        if chunk + 1 < CHUNKS:
            arrived[chunk] = after(arrived[chunk], sent)
        total = blocks[chunk]
        for value in arrived[chunk]:
            total += value.astype(F32) * grow_panel * grow_first
        for_z = lambda dest: lax.dynamic_index_in_dim(total, dest ^ (my_x & 1), 1, keepdims=False)
        other = (for_z(1 - my_zh) * shrink_first * shrink_panel).astype(WIRE)
        total = for_z(my_zh) + swap(other, "mem", 1).astype(F32) * grow_panel * grow_first
        results += [pick(my_core ^ core, [total[0], total[1]]) / (members - 1) for core in range(2)]
    return jnp.concatenate(results, axis=0)


def solution(mesh):
    in_specs = (P("samp", "mem"), P("samp", "mem"), P())
    out_specs = P("mem", "samp")
    return jax.shard_map(
        per_device, mesh=mesh, in_specs=in_specs, out_specs=out_specs, check_vma=False
    )
```

```python
import jax
import jax.numpy as jnp
from jax import lax
from jax.sharding import PartitionSpec as P

F32 = jnp.float32
BF16 = jnp.bfloat16
WIRE = jnp.float16
CHUNKS = 2


def swap(value, axis, bits):
    size = lax.axis_size(axis)
    return lax.ppermute(value, axis, [(i, i ^ bits) for i in range(size)])


def pick(index, options):
    result = options[-1]
    for i in range(len(options) - 2, -1, -1):
        result = jnp.where(index == i, options[i], result)
    return result


def row_stats(rows):
    wide = rows.astype(F32)
    return jnp.stack([jnp.sum(wide, -1), jnp.max(wide, -1), jnp.max(-wide, -1)])


def merge(parts):
    total = parts[0]
    for part in parts[1:]:
        total = jnp.concatenate([total[:1] + part[:1], jnp.maximum(total[1:], part[1:])])
    return total


def after(value, others):
    return lax.optimization_barrier((value, others))[0]


def per_device(first_plane, second_plane, panel_owner):
    samples, shard = first_plane.shape
    members = shard * lax.axis_size("mem")
    samp, mem = lax.axis_index("samp"), lax.axis_index("mem")
    my_x, my_z, my_core = samp >> 3, (samp >> 1) & 3, samp & 1
    my_y, my_zh = mem >> 1, mem & 1
    own_x, own_z, own_core = panel_owner >> 3, (panel_owner >> 1) & 3, panel_owner & 1

    by_x = second_plane.reshape(4, 128, shard)
    piece = lambda bits: lax.dynamic_index_in_dim(by_x, my_x ^ bits, 0, keepdims=False)
    from_x = [piece(0)] + [swap(piece(bits), "samp", 8 * bits) for bits in (1, 2, 3)]
    first_plane = after(first_plane, from_x[0])
    first_local = row_stats(first_plane)
    from_x = after(from_x, first_local)
    halves = [
        pick(my_x ^ own_x[p], from_x).reshape(CHUNKS, 2, 4, -1, shard) for p in range(2)
    ]
    half = lambda core: jnp.stack(
        [lax.dynamic_index_in_dim(h, core, 1, keepdims=False) for h in halves]
    )
    kept, got = half(my_core), swap(half(1 - my_core), "samp", 1)
    column = jnp.stack(
        [jnp.where(my_core == own_core[p], kept[p], got[p]) for p in range(2)]
    )
    eighth = column.shape[3]
    piece_z = lambda bits: lax.dynamic_index_in_dim(column, my_z ^ bits, 2, keepdims=False)
    from_z = [piece_z(0)] + [swap(piece_z(bits), "samp", 2 * bits) for bits in (1, 2, 3)]

    column_local = row_stats(column).reshape(3, -1)
    stats = jnp.concatenate([first_local, column_local], axis=1)
    stats = merge([stats] + [swap(stats, "mem", bits) for bits in (2, 4, 6)])
    stats = after(stats, from_z[1:])
    stats = merge([stats, swap(stats, "mem", 1)])
    mean, span = stats[0] / members, stats[1] + stats[2]
    first_mean = mean[:samples]
    facts = jnp.stack([mean[samples:], span[samples:]]).reshape((2,) + column.shape[:-1])

    mine = jnp.stack([pick(my_z ^ own_z[p], [f[p] for f in from_z]) for p in range(2)])
    parts = [mine] + [swap(mine, "samp", 2 * bits) for bits in (1, 2, 3)]
    facts = after(facts, parts[1])
    facts_z = [facts] + [swap(facts, "samp", 2 * bits) for bits in (1, 2, 3)]
    facts = jnp.stack([pick(my_z ^ own_z[p], [f[:, p] for f in facts_z]) for p in range(2)], 1)
    line = jnp.stack([pick(my_z ^ place, parts) for place in range(4)], 2)
    line = (line.astype(F32) - facts[0][..., None]).astype(BF16)
    tiles = 8
    bound = jnp.max(facts[1]) * 1.02
    mark = jnp.broadcast_to(bound, (1, eighth, shard)).astype(BF16)

    first_anom = (first_plane.astype(F32) - first_mean[:, None]).astype(BF16)
    rows = 4 * eighth
    gathered = []
    for chunk in range(CHUNKS):
        sent = line[:, chunk].reshape(tiles, eighth, shard)
        if chunk == 0:
            sent = jnp.concatenate([sent, mark])
        else:
            sent = after(sent, gathered[0][1])
        gathered.append([sent] + [swap(sent, "samp", 8 * bits) for bits in (1, 2, 3)])

    blocks, arrived = [], []
    for chunk in range(CHUNKS):
        if chunk > 0:
            gathered[chunk] = after(gathered[chunk], sent)
        near = jnp.stack(gathered[chunk])
        far = swap(near, "samp", 1)
        if chunk == 0:
            marks = jnp.stack([near[:, tiles, 0, :128], far[:, tiles, 0, :128]])
            shrink_first = 4.0 / jnp.maximum(jnp.max(span[:samples]), 1e-30)
            shrink_panel = 1.0 / jnp.maximum(jnp.max(marks.astype(F32)), 1e-30)
            grow_first, grow_panel = 1.0 / shrink_first, 1.0 / shrink_panel
        panel_anom = jnp.stack([near[:, :tiles], far[:, :tiles]])
        shares = lax.dot_general(
            panel_anom.reshape(16 * rows, shard),
            first_anom,
            (((1,), (1,)), ((), ())),
            preferred_element_type=F32,
        ).reshape(2, 2, 2, 2, rows, samples)

        def for_y(dest):
            start = (0, (dest & 1) ^ (my_x >> 1), 0, dest >> 1, 0, 0)
            block = lax.dynamic_slice(shares, start, (2, 1, 2, 1, rows, samples))
            return block.reshape(2, 2, rows, samples)

        sent = [
            (for_y(my_y ^ bits) * shrink_first * shrink_panel).astype(WIRE) for bits in (1, 2, 3)
        ]
        arrived.append([swap(sent[bits - 1], "mem", 2 * bits) for bits in (1, 2, 3)])
        blocks.append(for_y(my_y))

    results = []
    for chunk in range(CHUNKS):
        if chunk + 1 < CHUNKS:
            arrived[chunk] = after(arrived[chunk], sent)
        total = blocks[chunk]
        for value in arrived[chunk]:
            total += value.astype(F32) * grow_panel * grow_first
        for_z = lambda dest: lax.dynamic_index_in_dim(total, dest ^ (my_x & 1), 1, keepdims=False)
        other = (for_z(1 - my_zh) * shrink_first * shrink_panel).astype(WIRE)
        total = for_z(my_zh) + swap(other, "mem", 1).astype(F32) * grow_panel * grow_first
        results += [pick(my_core ^ core, [total[0], total[1]]) / (members - 1) for core in range(2)]
    return jnp.concatenate(results, axis=0)


def solution(mesh):
    in_specs = (P("samp", "mem"), P("samp", "mem"), P())
    out_specs = P("mem", "samp")
    return jax.shard_map(
        per_device, mesh=mesh, in_specs=in_specs, out_specs=out_specs, check_vma=False
    )
```

```python
import jax
import jax.numpy as jnp
from jax import lax
from jax.sharding import PartitionSpec as P

F32 = jnp.float32
BF16 = jnp.bfloat16
WIRE = jnp.float16
CHUNKS = 2


def swap(value, axis, bits):
    size = lax.axis_size(axis)
    return lax.ppermute(value, axis, [(i, i ^ bits) for i in range(size)])


def pick(index, options):
    result = options[-1]
    for i in range(len(options) - 2, -1, -1):
        result = jnp.where(index == i, options[i], result)
    return result


def row_stats(rows):
    wide = rows.astype(F32)
    return jnp.stack([jnp.sum(wide, -1), jnp.max(wide, -1), jnp.max(-wide, -1)])


def merge(parts):
    total = parts[0]
    for part in parts[1:]:
        total = jnp.concatenate([total[:1] + part[:1], jnp.maximum(total[1:], part[1:])])
    return total


def after(value, others):
    token, others = lax.optimization_barrier((lax.create_token(), others))
    return lax.optimization_barrier((token, value))[1], others


def beside(value, others):
    return lax.optimization_barrier((value, others))[0]


def per_device(first_plane, second_plane, panel_owner):
    samples, shard = first_plane.shape
    members = shard * lax.axis_size("mem")
    samp, mem = lax.axis_index("samp"), lax.axis_index("mem")
    my_x, my_z, my_core = samp >> 3, (samp >> 1) & 3, samp & 1
    my_y, my_zh = mem >> 1, mem & 1
    own_x, own_z, own_core = panel_owner >> 3, (panel_owner >> 1) & 3, panel_owner & 1

    by_x = second_plane.reshape(4, 128, shard)
    piece = lambda bits: lax.dynamic_index_in_dim(by_x, my_x ^ bits, 0, keepdims=False)
    from_x = [piece(0)] + [swap(piece(bits), "samp", 8 * bits) for bits in (1, 2, 3)]
    first_plane, from_x[0] = after(first_plane, from_x[0])
    first_local = row_stats(first_plane)
    from_x, first_local = after(from_x, first_local)
    halves = [
        pick(my_x ^ own_x[p], from_x).reshape(CHUNKS, 2, 4, -1, shard) for p in range(2)
    ]
    half = lambda core: jnp.stack(
        [lax.dynamic_index_in_dim(h, core, 1, keepdims=False) for h in halves]
    )
    kept, got = half(my_core), swap(half(1 - my_core), "samp", 1)
    column = jnp.stack(
        [jnp.where(my_core == own_core[p], kept[p], got[p]) for p in range(2)]
    )
    eighth = column.shape[3]
    piece_z = lambda bits: lax.dynamic_index_in_dim(column, my_z ^ bits, 2, keepdims=False)
    from_z = [piece_z(0)] + [swap(piece_z(bits), "samp", 2 * bits) for bits in (1, 2, 3)]

    column_local = row_stats(column).reshape(3, -1)
    stats = jnp.concatenate([first_local, column_local], axis=1)
    stats = merge([stats] + [swap(stats, "mem", bits) for bits in (2, 4, 6)])
    stats, from_z[1] = after(stats, from_z[1])
    stats = merge([stats, swap(stats, "mem", 1)])
    mean, span = stats[0] / members, stats[1] + stats[2]
    first_mean = mean[:samples]
    facts = jnp.stack([mean[samples:], span[samples:]]).reshape((2,) + column.shape[:-1])

    mine = jnp.stack([pick(my_z ^ own_z[p], [f[p] for f in from_z]) for p in range(2)])
    parts = [mine] + [swap(mine, "samp", 2 * bits) for bits in (1, 2, 3)]
    facts, parts[1] = after(facts, parts[1])
    facts_z = [facts] + [swap(facts, "samp", 2 * bits) for bits in (1, 2, 3)]
    facts = jnp.stack([pick(my_z ^ own_z[p], [f[:, p] for f in facts_z]) for p in range(2)], 1)
    line = jnp.stack([pick(my_z ^ place, parts) for place in range(4)], 2)
    line = (line.astype(F32) - facts[0][..., None]).astype(BF16)
    tiles = 8
    bound = jnp.max(facts[1]) * 1.02
    mark = jnp.broadcast_to(bound, (1, eighth, shard)).astype(BF16)

    first_anom = (first_plane.astype(F32) - first_mean[:, None]).astype(BF16)
    gathered = []
    for chunk in range(CHUNKS):
        sent = line[:, chunk].reshape(tiles, eighth, shard)
        if chunk == 0:
            sent = jnp.concatenate([sent, mark])
        else:
            sent = beside(sent, gathered[0][1])
        gathered.append([sent] + [swap(sent, "samp", 8 * bits) for bits in (1, 2, 3)])

    gathered[0], first_anom = after(gathered[0], first_anom)
    blocks, arrived = [], []
    for chunk in range(CHUNKS):
        if chunk > 0:
            gathered[chunk] = beside(gathered[chunk], sent)
        near = jnp.stack(gathered[chunk])
        panel_anom = jnp.stack([near, swap(near, "samp", 1)])
        if chunk == 0:
            marks = panel_anom[:, :, tiles, 0, :128].astype(F32)
            shrink_first = 4.0 / jnp.maximum(jnp.max(span[:samples]), 1e-30)
            shrink_panel = 1.0 / jnp.maximum(jnp.max(marks), 1e-30)
            grow_first, grow_panel = 1.0 / shrink_first, 1.0 / shrink_panel
        height = panel_anom.shape[2]
        shares = lax.dot_general(
            panel_anom.reshape(-1, shard),
            first_anom,
            (((1,), (1,)), ((), ())),
            preferred_element_type=F32,
        ).reshape(2, 2, 2, height, eighth, samples)

        def for_y(dest):
            start = (0, (dest & 1) ^ (my_x >> 1), 0, 4 * (dest >> 1), 0, 0)
            block = lax.dynamic_slice(shares, start, (2, 1, 2, 4, eighth, samples))
            return block.reshape(2, 2, 4, eighth, samples)

        sent = [
            (for_y(my_y ^ bits) * shrink_first * shrink_panel).astype(WIRE) for bits in (1, 2, 3)
        ]
        arrived.append([swap(sent[bits - 1], "mem", 2 * bits) for bits in (1, 2, 3)])
        blocks.append(for_y(my_y))

    results = []
    for chunk in range(CHUNKS):
        if chunk + 1 < CHUNKS:
            arrived[chunk] = beside(arrived[chunk], sent)

        def for_z(dest):
            part = lambda v: lax.dynamic_index_in_dim(v, dest ^ (my_x & 1), 1, keepdims=False)
            total = part(blocks[chunk])
            for value in arrived[chunk]:
                total += part(value).astype(F32) * grow_panel * grow_first
            return total

        other = (for_z(1 - my_zh) * shrink_first * shrink_panel).astype(WIRE)
        total = for_z(my_zh) + swap(other, "mem", 1).astype(F32) * grow_panel * grow_first
        results += [pick(my_core ^ core, [total[0], total[1]]) / (members - 1) for core in range(2)]
    return jnp.stack(results).reshape(-1, samples)


def solution(mesh):
    in_specs = (P("samp", "mem"), P("samp", "mem"), P())
    out_specs = P("mem", "samp")
    return jax.shard_map(
        per_device, mesh=mesh, in_specs=in_specs, out_specs=out_specs, check_vma=False
    )
```

```python
import jax
import jax.numpy as jnp
from jax import lax
from jax.sharding import PartitionSpec as P

F32 = jnp.float32
BF16 = jnp.bfloat16
WIRE = jnp.float16


def swap(value, axis, bits):
    size = lax.axis_size(axis)
    return lax.ppermute(value, axis, [(i, i ^ bits) for i in range(size)])


def pick(index, options):
    result = options[-1]
    for i in range(len(options) - 2, -1, -1):
        result = jnp.where(index == i, options[i], result)
    return result


def row_stats(rows):
    wide = rows.astype(F32)
    return jnp.stack([jnp.sum(wide, -1), jnp.max(wide, -1), jnp.max(-wide, -1)])


def merge(parts):
    total = parts[0]
    for part in parts[1:]:
        total = jnp.concatenate([total[:1] + part[:1], jnp.maximum(total[1:], part[1:])])
    return total


def after(value, others):
    token, others = lax.optimization_barrier((lax.create_token(), others))
    return lax.optimization_barrier((token, value))[1], others


def per_device(first_plane, second_plane, panel_owner):
    samples, shard = first_plane.shape
    members = shard * lax.axis_size("mem")
    samp, mem = lax.axis_index("samp"), lax.axis_index("mem")
    my_x, my_z, my_core = samp >> 3, (samp >> 1) & 3, samp & 1
    my_y, my_zh = mem >> 1, mem & 1
    own_x, own_z, own_core = panel_owner >> 3, (panel_owner >> 1) & 3, panel_owner & 1

    by_x = second_plane.reshape(4, 128, shard)
    piece = lambda bits: lax.dynamic_index_in_dim(by_x, my_x ^ bits, 0, keepdims=False)
    from_x = [piece(0)] + [swap(piece(bits), "samp", 8 * bits) for bits in (1, 2, 3)]
    first_plane, from_x[0] = after(first_plane, from_x[0])
    first_local = row_stats(first_plane)
    from_x, first_local = after(from_x, first_local)
    halves = [
        pick(my_x ^ own_x[p], from_x).reshape(2, 4, 2, 8, shard) for p in range(2)
    ]
    half = lambda core: jnp.stack(
        [lax.dynamic_index_in_dim(h, core, 0, keepdims=False) for h in halves]
    )
    kept, got = half(my_core), swap(half(1 - my_core), "samp", 1)
    column = jnp.stack(
        [jnp.where(my_core == own_core[p], kept[p], got[p]) for p in range(2)]
    )
    piece_z = lambda bits: lax.dynamic_index_in_dim(column, my_z ^ bits, 1, keepdims=False)
    from_z = [piece_z(0)] + [swap(piece_z(bits), "samp", 2 * bits) for bits in (1, 2, 3)]

    column_local = row_stats(column).reshape(3, -1)
    stats = jnp.concatenate([first_local, column_local], axis=1)
    stats = merge([stats] + [swap(stats, "mem", bits) for bits in (2, 4, 6)])
    stats, from_z[1] = after(stats, from_z[1])
    stats = merge([stats, swap(stats, "mem", 1)])
    mean, span = stats[0] / members, stats[1] + stats[2]
    first_mean = mean[:samples]
    facts = jnp.stack([mean[samples:], span[samples:]]).reshape((2,) + column.shape[:-1])

    mine = jnp.stack([pick(my_z ^ own_z[p], [f[p] for f in from_z]) for p in range(2)])
    parts = [mine] + [swap(mine, "samp", 2 * bits) for bits in (1, 2, 3)]
    facts, parts[1] = after(facts, parts[1])
    facts_z = [facts] + [swap(facts, "samp", 2 * bits) for bits in (1, 2, 3)]
    facts = jnp.stack([pick(my_z ^ own_z[p], [f[:, p] for f in facts_z]) for p in range(2)], 1)
    line = jnp.stack([pick(my_z ^ place, parts) for place in range(4)], 1)
    line = (line.astype(F32) - facts[0][..., None]).astype(BF16)
    tiles = 16
    bound = jnp.max(facts[1]) * 1.02
    mark = jnp.broadcast_to(bound, (1, 8, shard)).astype(BF16)
    sent = jnp.concatenate([line.reshape(tiles, 8, shard), mark])
    near = jnp.stack([sent] + [swap(sent, "samp", 8 * bits) for bits in (1, 2, 3)])
    far = swap(near, "samp", 1)

    first_anom = (first_plane.astype(F32) - first_mean[:, None]).astype(BF16)
    shrink_first = 4.0 / jnp.maximum(jnp.max(span[:samples]), 1e-30)
    grow_first = 1.0 / shrink_first
    results = []
    for anom in (near, far):
        shrink_panel = 1.0 / jnp.maximum(jnp.max(anom[:, tiles, 0, :128].astype(F32)), 1e-30)
        grow_panel = 1.0 / shrink_panel
        shares = lax.dot_general(
            anom.reshape(-1, shard),
            first_anom,
            (((1,), (1,)), ((), ())),
            preferred_element_type=F32,
        ).reshape(2, 2, tiles + 1, 8, samples)

        def for_y(dest):
            start = ((dest & 1) ^ (my_x >> 1), 0, 8 * (dest >> 1), 0, 0)
            block = lax.dynamic_slice(shares, start, (1, 2, 8, 8, samples))
            return block.reshape(2, 8, 8, samples)

        blocks = [for_y(my_y)]
        for bits in (1, 2, 3):
            sent = (for_y(my_y ^ bits) * shrink_first * shrink_panel).astype(WIRE)
            blocks.append(swap(sent, "mem", 2 * bits))

        def for_z(dest):
            part = lambda v: lax.dynamic_index_in_dim(v, dest ^ (my_x & 1), 0, keepdims=False)
            total = part(blocks[0])
            for value in blocks[1:]:
                total += part(value).astype(F32) * grow_panel * grow_first
            return total

        other = (for_z(1 - my_zh) * shrink_first * shrink_panel).astype(WIRE)
        total = for_z(my_zh) + swap(other, "mem", 1).astype(F32) * grow_panel * grow_first
        results.append(total / (members - 1))
    return jnp.stack([pick(my_core ^ core, results) for core in range(2)]).reshape(-1, samples)


def solution(mesh):
    in_specs = (P("samp", "mem"), P("samp", "mem"), P())
    out_specs = P("mem", "samp")
    return jax.shard_map(
        per_device, mesh=mesh, in_specs=in_specs, out_specs=out_specs, check_vma=False
    )
```

```python
import jax
import jax.numpy as jnp
from jax import lax
from jax.sharding import PartitionSpec as P

F32 = jnp.float32
BF16 = jnp.bfloat16
WIRE = jnp.float16


def swap(value, axis, bits):
    size = lax.axis_size(axis)
    return lax.ppermute(value, axis, [(i, i ^ bits) for i in range(size)])


def pick(index, options):
    result = options[-1]
    for i in range(len(options) - 2, -1, -1):
        result = jnp.where(index == i, options[i], result)
    return result


def row_stats(rows):
    wide = rows.astype(F32)
    return jnp.stack([jnp.sum(wide, -1), jnp.max(wide, -1), jnp.max(-wide, -1)])


def merge(parts):
    total = parts[0]
    for part in parts[1:]:
        total = jnp.concatenate([total[:1] + part[:1], jnp.maximum(total[1:], part[1:])])
    return total


def after(value, others):
    token, others = lax.optimization_barrier((lax.create_token(), others))
    return lax.optimization_barrier((token, value))[1], others


def per_device(first_plane, second_plane, panel_owner):
    samples, shard = first_plane.shape
    members = shard * lax.axis_size("mem")
    samp, mem = lax.axis_index("samp"), lax.axis_index("mem")
    my_x, my_z, my_core = samp >> 3, (samp >> 1) & 3, samp & 1
    my_y, my_zh = mem >> 1, mem & 1
    own_x, own_z, own_core = panel_owner >> 3, (panel_owner >> 1) & 3, panel_owner & 1

    by_x = second_plane.reshape(4, 128, shard)
    piece = lambda bits: lax.dynamic_index_in_dim(by_x, my_x ^ bits, 0, keepdims=False)
    from_x = [piece(0)] + [swap(piece(bits), "samp", 8 * bits) for bits in (1, 2, 3)]
    first_plane, from_x[0] = after(first_plane, from_x[0])
    first_local = row_stats(first_plane)
    from_x, first_local = after(from_x, first_local)
    halves = [
        pick(my_x ^ own_x[p], from_x).reshape(2, 4, 2, 8, shard) for p in range(2)
    ]
    half = lambda core: jnp.stack(
        [lax.dynamic_index_in_dim(h, core, 0, keepdims=False) for h in halves]
    )
    kept, got = half(my_core), swap(half(1 - my_core), "samp", 1)
    column = jnp.stack(
        [jnp.where(my_core == own_core[p], kept[p], got[p]) for p in range(2)]
    )
    piece_z = lambda bits: lax.dynamic_index_in_dim(column, my_z ^ bits, 1, keepdims=False)
    from_z = [piece_z(0)] + [swap(piece_z(bits), "samp", 2 * bits) for bits in (1, 2, 3)]

    column_local = row_stats(column).reshape(3, -1)
    stats = jnp.concatenate([first_local, column_local], axis=1)
    stats = merge([stats] + [swap(stats, "mem", bits) for bits in (2, 4, 6)])
    stats, from_z[1] = after(stats, from_z[1])
    stats = merge([stats, swap(stats, "mem", 1)])
    mean, span = stats[0] / members, stats[1] + stats[2]
    first_mean = mean[:samples]
    facts = jnp.stack([mean[samples:], span[samples:]]).reshape((2,) + column.shape[:-1])

    mine = jnp.stack([pick(my_z ^ own_z[p], [f[p] for f in from_z]) for p in range(2)])
    parts = [mine] + [swap(mine, "samp", 2 * bits) for bits in (1, 2, 3)]
    facts_z = [facts] + [swap(facts, "samp", 2 * bits) for bits in (1, 2, 3)]
    facts = jnp.stack([pick(my_z ^ own_z[p], [f[:, p] for f in facts_z]) for p in range(2)], 1)
    line = jnp.stack([pick(my_z ^ place, parts) for place in range(4)], 1)
    sent = line.reshape(16, 8, shard)
    near = jnp.stack([sent] + [swap(sent, "samp", 8 * bits) for bits in (1, 2, 3)])
    far = swap(near, "samp", 1)
    near_facts = jnp.stack([facts] + [swap(facts, "samp", 8 * bits) for bits in (1, 2, 3)])
    far_facts = swap(near_facts, "samp", 1)

    first_anom = (first_plane.astype(F32) - first_mean[:, None]).astype(BF16)
    shrink_first = 4.0 / jnp.maximum(jnp.max(span[:samples]), 1e-30)
    grow_first = 1.0 / shrink_first
    out = jnp.zeros((2, 8, 8, samples), F32)
    for place, rows, its_facts in ((my_core, near, near_facts), (1 - my_core, far, far_facts)):
        shrink_panel = 1.0 / jnp.maximum(jnp.max(its_facts[:, 1]), 1e-30)
        grow_panel = 1.0 / shrink_panel
        means = its_facts[:, 0].reshape(4, 16, 8, 1)
        anom = (rows.astype(F32) - means).astype(BF16)
        shares = lax.dot_general(
            anom.reshape(-1, shard),
            first_anom,
            (((1,), (1,)), ((), ())),
            preferred_element_type=F32,
        ).reshape(2, 2, 16, 8, samples)

        def for_y(dest):
            start = ((dest & 1) ^ (my_x >> 1), 0, 8 * (dest >> 1), 0, 0)
            block = lax.dynamic_slice(shares, start, (1, 2, 8, 8, samples))
            return block.reshape(2, 8, 8, samples)

        blocks = [for_y(my_y)]
        for bits in (1, 2, 3):
            sent = (for_y(my_y ^ bits) * shrink_first * shrink_panel).astype(WIRE)
            blocks.append(swap(sent, "mem", 2 * bits))

        def for_z(dest):
            part = lambda v: lax.dynamic_index_in_dim(v, dest ^ (my_x & 1), 0, keepdims=False)
            total = part(blocks[0])
            for value in blocks[1:]:
                total += part(value).astype(F32) * grow_panel * grow_first
            return total

        other = (for_z(1 - my_zh) * shrink_first * shrink_panel).astype(WIRE)
        total = for_z(my_zh) + swap(other, "mem", 1).astype(F32) * grow_panel * grow_first
        out = lax.dynamic_update_index_in_dim(out, total / (members - 1), place, 0)
    return out.reshape(-1, samples)


def solution(mesh):
    in_specs = (P("samp", "mem"), P("samp", "mem"), P())
    out_specs = P("mem", "samp")
    return jax.shard_map(
        per_device, mesh=mesh, in_specs=in_specs, out_specs=out_specs, check_vma=False
    )
```

```python
import jax
import jax.numpy as jnp
from jax import lax
from jax.sharding import PartitionSpec as P

F32 = jnp.float32
BF16 = jnp.bfloat16
WIRE = jnp.float16


def swap(value, axis, bits):
    size = lax.axis_size(axis)
    return lax.ppermute(value, axis, [(i, i ^ bits) for i in range(size)])


def pick(index, options):
    result = options[-1]
    for i in range(len(options) - 2, -1, -1):
        result = jnp.where(index == i, options[i], result)
    return result


def row_stats(rows):
    wide = rows.astype(F32)
    return jnp.stack([jnp.sum(wide, -1), jnp.max(wide, -1), jnp.max(-wide, -1)])


def merge(parts):
    total = parts[0]
    for part in parts[1:]:
        total = jnp.concatenate([total[:1] + part[:1], jnp.maximum(total[1:], part[1:])])
    return total


def after(value, others):
    token, others = lax.optimization_barrier((lax.create_token(), others))
    return lax.optimization_barrier((token, value))[1], others


def per_device(first_plane, second_plane, panel_owner):
    samples, shard = first_plane.shape
    members = shard * lax.axis_size("mem")
    samp, mem = lax.axis_index("samp"), lax.axis_index("mem")
    my_x, my_z, my_core = samp >> 3, (samp >> 1) & 3, samp & 1
    my_y, my_zh = mem >> 1, mem & 1
    own_x, own_z, own_core = panel_owner >> 3, (panel_owner >> 1) & 3, panel_owner & 1

    by_x = second_plane.reshape(4, 128, shard)
    piece = lambda bits: lax.dynamic_index_in_dim(by_x, my_x ^ bits, 0, keepdims=False)
    from_x = [piece(0)] + [swap(piece(bits), "samp", 8 * bits) for bits in (1, 2, 3)]
    first_plane, from_x[0] = after(first_plane, from_x[0])
    first_local = row_stats(first_plane)
    from_x, first_local = after(from_x, first_local)
    halves = [
        pick(my_x ^ own_x[p], from_x).reshape(2, 4, 2, 8, shard) for p in range(2)
    ]
    half = lambda core: jnp.stack(
        [lax.dynamic_index_in_dim(h, core, 0, keepdims=False) for h in halves]
    )
    kept, got = half(my_core), swap(half(1 - my_core), "samp", 1)
    column = jnp.stack(
        [jnp.where(my_core == own_core[p], kept[p], got[p]) for p in range(2)]
    )
    piece_z = lambda bits: lax.dynamic_index_in_dim(column, my_z ^ bits, 1, keepdims=False)
    from_z = [piece_z(0)] + [swap(piece_z(bits), "samp", 2 * bits) for bits in (1, 2, 3)]

    column_local = row_stats(column).reshape(3, -1)
    stats = jnp.concatenate([first_local, column_local], axis=1)
    stats = merge([stats] + [swap(stats, "mem", bits) for bits in (2, 4, 6)])
    stats, from_z[1] = after(stats, from_z[1])
    stats = merge([stats, swap(stats, "mem", 1)])
    mean, span = stats[0] / members, stats[1] + stats[2]
    first_mean = mean[:samples]
    facts = jnp.stack([mean[samples:], span[samples:]]).reshape((2,) + column.shape[:-1])

    mine = jnp.stack([pick(my_z ^ own_z[p], [f[p] for f in from_z]) for p in range(2)])
    parts = [mine] + [swap(mine, "samp", 2 * bits) for bits in (1, 2, 3)]
    facts, parts[1] = after(facts, parts[1])
    facts_z = [facts] + [swap(facts, "samp", 2 * bits) for bits in (1, 2, 3)]
    shrink_first = 4.0 / jnp.maximum(jnp.max(span[:samples]), 1e-30)
    facts_z[1], shrink_first = after(facts_z[1], shrink_first)
    facts = jnp.stack([pick(my_z ^ own_z[p], [f[:, p] for f in facts_z]) for p in range(2)], 1)
    line = jnp.stack([pick(my_z ^ place, parts) for place in range(4)], 1)
    line = (line.astype(F32) - facts[0][..., None]).astype(BF16)
    tiles = 16
    bound = jnp.max(facts[1]) * 1.02
    mark = jnp.broadcast_to(bound, (1, 8, shard)).astype(BF16)
    sent = jnp.concatenate([line.reshape(tiles, 8, shard), mark])
    near = jnp.stack([sent] + [swap(sent, "samp", 8 * bits) for bits in (1, 2, 3)])
    far = swap(near, "samp", 1)

    first_anom = (first_plane.astype(F32) - first_mean[:, None]).astype(BF16)
    grow_first = 1.0 / shrink_first
    give, keep = (1 - my_zh) ^ (my_x & 1), my_zh ^ (my_x & 1)
    out = jnp.zeros((2, 8, 8, samples), F32)
    for place, anom in ((my_core, near), (1 - my_core, far)):
        shrink_panel = 1.0 / jnp.maximum(jnp.max(anom[:, tiles, 0, :128].astype(F32)), 1e-30)
        grow_panel = 1.0 / shrink_panel
        shares = lax.dot_general(
            anom.reshape(-1, shard),
            first_anom,
            (((1,), (1,)), ((), ())),
            preferred_element_type=F32,
        ).reshape(2, 2, tiles + 1, 8, samples)

        def block(dest, low, lows):
            start = ((dest & 1) ^ (my_x >> 1), low, 8 * (dest >> 1), 0, 0)
            return lax.dynamic_slice(shares, start, (1, lows, 8, 8, samples))[0]

        def over_y(low, lows):
            parts = [block(my_y, low, lows)]
            for bits in (1, 2, 3):
                sent = block(my_y ^ bits, low, lows) * shrink_first * shrink_panel
                parts.append(swap(sent.astype(WIRE), "mem", 2 * bits))
            return parts

        def total(parts):
            result = parts[0]
            for value in parts[1:]:
                result += value.astype(F32) * grow_panel * grow_first
            return result

        if anom is far:
            given, kept = [[v[0] for v in over_y(low, 1)] for low in (give, keep)]
        else:
            both = over_y(0, 2)
            given, kept = [
                [lax.dynamic_index_in_dim(v, low, 0, keepdims=False) for v in both]
                for low in (give, keep)
            ]
        given = (total(given) * shrink_first * shrink_panel).astype(WIRE)
        result = total(kept + [swap(given, "mem", 1)]) / (members - 1)
        out = lax.dynamic_update_index_in_dim(out, result, place, 0)
    return out.reshape(-1, samples)


def solution(mesh):
    in_specs = (P("samp", "mem"), P("samp", "mem"), P())
    out_specs = P("mem", "samp")
    return jax.shard_map(
        per_device, mesh=mesh, in_specs=in_specs, out_specs=out_specs, check_vma=False
    )
```

```python
import jax
import jax.numpy as jnp
from jax import lax
from jax.sharding import PartitionSpec as P

F32 = jnp.float32
BF16 = jnp.bfloat16
WIRE = jnp.float16


def swap(value, axis, bits):
    size = lax.axis_size(axis)
    return lax.ppermute(value, axis, [(i, i ^ bits) for i in range(size)])


def pick(index, options):
    result = options[-1]
    for i in range(len(options) - 2, -1, -1):
        result = jnp.where(index == i, options[i], result)
    return result


def row_stats(rows):
    wide = rows.astype(F32)
    return jnp.stack([jnp.sum(wide, -1), jnp.max(wide, -1), jnp.max(-wide, -1)])


def merge(parts):
    total = parts[0]
    for part in parts[1:]:
        total = jnp.concatenate([total[:1] + part[:1], jnp.maximum(total[1:], part[1:])])
    return total


def after(value, others):
    token, others = lax.optimization_barrier((lax.create_token(), others))
    return lax.optimization_barrier((token, value))[1], others


def per_device(first_plane, second_plane, panel_owner):
    samples, shard = first_plane.shape
    members = shard * lax.axis_size("mem")
    samp, mem = lax.axis_index("samp"), lax.axis_index("mem")
    my_x, my_z, my_core = samp >> 3, (samp >> 1) & 3, samp & 1
    my_y, my_zh = mem >> 1, mem & 1
    own_x, own_z, own_core = panel_owner >> 3, (panel_owner >> 1) & 3, panel_owner & 1

    by_x = second_plane.reshape(4, 128, shard)
    piece = lambda bits: lax.dynamic_index_in_dim(by_x, my_x ^ bits, 0, keepdims=False)
    from_x = [piece(0)] + [swap(piece(bits), "samp", 8 * bits) for bits in (1, 2, 3)]
    first_plane, from_x[0] = after(first_plane, from_x[0])
    first_local = row_stats(first_plane)
    from_x, first_local = after(from_x, first_local)
    halves = [
        pick(my_x ^ own_x[p], from_x).reshape(2, 4, 2, 8, shard) for p in range(2)
    ]
    half = lambda core: jnp.stack(
        [lax.dynamic_index_in_dim(h, core, 0, keepdims=False) for h in halves]
    )
    kept, got = half(my_core), swap(half(1 - my_core), "samp", 1)
    column = jnp.stack(
        [jnp.where(my_core == own_core[p], kept[p], got[p]) for p in range(2)]
    )
    piece_z = lambda bits: lax.dynamic_index_in_dim(column, my_z ^ bits, 1, keepdims=False)
    from_z = [piece_z(0)] + [swap(piece_z(bits), "samp", 2 * bits) for bits in (1, 2, 3)]

    column_local = row_stats(column).reshape(3, -1)
    stats = jnp.concatenate([first_local, column_local], axis=1)
    stats = merge([stats] + [swap(stats, "mem", bits) for bits in (2, 4, 6)])
    stats, from_z[1] = after(stats, from_z[1])
    stats = merge([stats, swap(stats, "mem", 1)])
    mean, span = stats[0] / members, stats[1] + stats[2]
    first_mean = mean[:samples]
    facts = jnp.stack([mean[samples:], span[samples:]]).reshape((2,) + column.shape[:-1])

    mine = jnp.stack([pick(my_z ^ own_z[p], [f[p] for f in from_z]) for p in range(2)])
    parts = [mine] + [swap(mine, "samp", 2 * bits) for bits in (1, 2, 3)]
    facts, parts[1] = after(facts, parts[1])
    facts_z = [facts] + [swap(facts, "samp", 2 * bits) for bits in (1, 2, 3)]
    shrink_first = 4.0 / jnp.maximum(jnp.max(span[:samples]), 1e-30)
    facts_z[1], shrink_first = after(facts_z[1], shrink_first)
    facts = jnp.stack([pick(my_z ^ own_z[p], [f[:, p] for f in facts_z]) for p in range(2)], 1)
    line = jnp.stack([pick(my_z ^ place, parts) for place in range(4)], 1)
    line = (line.astype(F32) - facts[0][..., None]).astype(BF16)
    tiles = 16
    bound = jnp.max(facts[1]) * 1.02
    mark = jnp.broadcast_to(bound, (1, 8, shard)).astype(BF16)
    sent = jnp.concatenate([line.reshape(tiles, 8, shard), mark])
    near = jnp.stack([sent] + [swap(sent, "samp", 8 * bits) for bits in (1, 2, 3)])
    far = swap(near, "samp", 1)

    first_anom = (first_plane.astype(F32) - first_mean[:, None]).astype(BF16)
    grow_first = 1.0 / shrink_first
    give, keep = (1 - my_zh) ^ (my_x & 1), my_zh ^ (my_x & 1)
    out = jnp.zeros((2, 8, 8, samples), F32)
    for place, anom in ((my_core, near), (1 - my_core, far)):
        shrink_panel = 1.0 / jnp.maximum(jnp.max(anom[:, tiles, 0, :128].astype(F32)), 1e-30)
        grow_panel = 1.0 / shrink_panel
        shares = lax.dot_general(
            anom.reshape(-1, shard),
            first_anom,
            (((1,), (1,)), ((), ())),
            preferred_element_type=F32,
        ).reshape(2, 2, tiles + 1, 8, samples)

        def block(dest, low, lows):
            start = ((dest & 1) ^ (my_x >> 1), low, 8 * (dest >> 1), 0, 0)
            return lax.dynamic_slice(shares, start, (1, lows, 8, 8, samples))[0]

        def over_y(low, lows):
            parts = [block(my_y, low, lows)]
            for bits in (2, 1, 3):
                sent = block(my_y ^ bits, low, lows) * shrink_first * shrink_panel
                parts.append(swap(sent.astype(WIRE), "mem", 2 * bits))
            return parts

        def total(parts):
            result = parts[0]
            for value in parts[1:]:
                result += value.astype(F32) * grow_panel * grow_first
            return result

        if anom is far:
            given, kept = [[v[0] for v in over_y(low, 1)] for low in (give, keep)]
        else:
            both = over_y(0, 2)
            given, kept = [
                [lax.dynamic_index_in_dim(v, low, 0, keepdims=False) for v in both]
                for low in (give, keep)
            ]
        given = (total(given) * shrink_first * shrink_panel).astype(WIRE)
        result = total(kept + [swap(given, "mem", 1)]) / (members - 1)
        out = lax.dynamic_update_index_in_dim(out, result, place, 0)
    return out.reshape(-1, samples)


def solution(mesh):
    in_specs = (P("samp", "mem"), P("samp", "mem"), P())
    out_specs = P("mem", "samp")
    return jax.shard_map(
        per_device, mesh=mesh, in_specs=in_specs, out_specs=out_specs, check_vma=False
    )
```
